512 devices in a mesh: dp: 32 (over z, x_hi, core), tensor: 16 (over x_lo, y).
Axes of the slice: x: 4 (x_hi: 2, x_lo: 2; x = x_hi * 2 + x_lo), y: 8, z: 8, core: 2. Of those that a mesh axis runs over, the one named last changes fastest.
Arguments:
- gate_pre: bfloat16 [4096, 14336], P('dp', 'tensor'), may hold values from -6 to 6
- up_pre: bfloat16 [4096, 14336], P('dp', 'tensor'), may hold values from -6 to 6
- cotangent: bfloat16 [4096, 4096], P('dp', 'tensor'), may hold values from -6 to 6
- weight_tiles: bfloat16 [16, 96, 128, 128], P('tensor', 'dp'), may hold values from -0.109375 to 0.109375
- tile_slots: int32 [16, 96], P('tensor', 'dp'), may hold values from 0 to 223, as said below
- live_counts: int32 [16], P('tensor'), may hold values from 24 to 96, as said below
Outputs:
- projected: bfloat16 [4096, 4096], P('dp', 'tensor')
- gate_grad: bfloat16 [4096, 14336], P('dp', 'tensor')
- up_grad: bfloat16 [4096, 14336], P('dp', 'tensor')
- tile_grad: float32 [16, 96, 128, 128], P('tensor', 'dp')
The draws below stay inside these ranges and needn't reach their ends.
Inputs may be any that keep to these rules, and one draw needn't show every extreme that they name: `tile_slots`: within one tensor shard all 96 entries are distinct. `live_counts`: some shard has all 96 slots live.
All inputs are finite; a program needn't handle non-finite values.
Results may differ from the reference program's by a relative error of at most 0.019.
Values may be sent and summed in bfloat16 or wider, within the bound.
A program may use at most 64 MiB of HBM per device.

```python
import jax
import jax.numpy as jnp
from jax import lax

D = 4096
FF = 14336
BLOCK = 128
CAP = 96
TOK = 128
TOKENS = 4096
HID_BLOCKS = 7
MODEL_BLOCKS = 32
N_DP = 32
N_TENSOR = 16


def draw_tile_slots(key, part):
    shard_keys = jax.random.split(jax.random.fold_in(key, 3), N_TENSOR)

    def shard_perm(shard_key):
        return jax.random.permutation(shard_key, HID_BLOCKS * MODEL_BLOCKS)[:CAP]
    return jax.vmap(shard_perm)(shard_keys).astype(jnp.int32)


def draw_live_counts(key, part):
    lowest = CAP // 4
    values = jax.random.randint(jax.random.fold_in(key, 1), (N_TENSOR,), lowest, CAP + 1)
    full_shard = jax.random.randint(jax.random.fold_in(key, 2), (), 0, N_TENSOR)
    return jnp.where(jnp.arange(N_TENSOR) == full_shard, CAP, values).astype(jnp.int32)


def levels(rng, extent, cuts, low, high):
    level, own = 1.0, jax.random.fold_in(rng, 6)
    for dim, shards_of in cuts:
        heights = jnp.exp(jax.random.uniform(jax.random.fold_in(own, dim), (shards_of,), jnp.float32, low / len(cuts), high / len(cuts)))
        level = level * jnp.repeat(heights, extent[dim] // shards_of).reshape([-1 if axis == dim else 1 for axis in range(len(extent))])
    return level


def centred(key, extent, scale, limit, cuts=(), held_as=jnp.bfloat16):
    array = jax.random.normal(key, extent, jnp.float32) * scale
    if len(cuts) > 0:
        array = levels(key, extent, cuts, -0.22, 0.18) * array
    return jnp.clip(array, min=-limit, max=limit).astype(held_as)


def setup_inputs(seed: int = 0) -> dict:
    arg_keys = jax.random.split(jax.random.key(seed), 7)
    gate_pre = centred(arg_keys[0], (TOKENS, FF), 1.0, 6.0, ((0, 32), (1, 16)))
    up_pre = centred(arg_keys[1], (TOKENS, FF), 1.0, 6.0, ((0, 32), (1, 16)))
    cotangent = centred(arg_keys[2], (TOKENS, D), 1.0, 6.0, ((0, 32), (1, 16)))
    weight_tiles = centred(arg_keys[3], (N_TENSOR, CAP, BLOCK, BLOCK), (BLOCK * N_TENSOR * CAP // (2 * MODEL_BLOCKS)) ** -0.5, 0.109375, ((0, 16), (1, 32)))
    tile_slots = draw_tile_slots(jax.random.fold_in(arg_keys[6], 71), 0)
    live_counts = draw_live_counts(jax.random.fold_in(arg_keys[6], 71), 0)
    return dict(gate_pre=gate_pre, up_pre=up_pre, cotangent=cotangent, weight_tiles=weight_tiles, tile_slots=tile_slots, live_counts=live_counts)


def reference(gate_pre, up_pre, cotangent, weight_tiles, tile_slots, live_counts):
    shards = N_TENSOR
    hid_width = FF // shards
    group_size = 16
    groups = CAP // group_size
    token_scale = TOKENS ** -0.5
    gate_all = gate_pre.astype(jnp.float32)
    up_all = up_pre.astype(jnp.float32)
    hidden = (gate_all * jax.nn.sigmoid(gate_all) * up_all).astype(jnp.bfloat16)
    hid_shards = hidden.reshape(TOKENS, shards, HID_BLOCKS, BLOCK).transpose(1, 2, 0, 3)
    cot_blocks = cotangent.reshape(TOKENS, MODEL_BLOCKS, BLOCK).transpose(1, 0, 2)
    gate_shards = gate_pre.reshape(TOKENS, shards, hid_width).transpose(1, 0, 2)
    up_shards = up_pre.reshape(TOKENS, shards, hid_width).transpose(1, 0, 2)

    def shard_step(running, shard_data):
        hid_blocks, shard_tiles, shard_slots, live_count, gate_part, up_part = shard_data

        def group_step(state_pair, group_data):
            part_sum, hidden_grad = state_pair
            group_tiles, group_slots, offset = group_data
            is_live = (offset + jnp.arange(group_size, dtype=jnp.int32)) < live_count
            hid_index = (group_slots // MODEL_BLOCKS).astype(jnp.int32)
            mod_index = (group_slots % MODEL_BLOCKS).astype(jnp.int32)
            picked = hid_blocks[hid_index].astype(jnp.float32)
            cot_picked = cot_blocks[mod_index].astype(jnp.float32)
            weights = jnp.where(is_live[:, None, None], group_tiles.astype(jnp.float32), 0.0)
            part_sum = part_sum.at[mod_index].add(jnp.einsum('gtb,gbc->gtc', picked, weights))
            hidden_grad = hidden_grad.at[hid_index].add(jnp.einsum('gtc,gbc->gtb', cot_picked, weights))
            tile_terms = jnp.einsum('gdtb,gdtc->gdbc', picked.reshape(group_size, N_DP, TOK, BLOCK),
                                    cot_picked.reshape(group_size, N_DP, TOK, BLOCK)) * token_scale
            tile_terms = jnp.where(is_live[:, None, None, None], tile_terms, 0.0)
            rounded = lax.optimization_barrier(tile_terms.astype(jnp.bfloat16)).astype(jnp.float32)
            return (part_sum, hidden_grad), jnp.sum(rounded, axis=1)

        offsets = jnp.arange(groups, dtype=jnp.int32) * group_size
        initial = (jnp.zeros((MODEL_BLOCKS, TOKENS, BLOCK), jnp.float32),
                   jnp.zeros((HID_BLOCKS, TOKENS, BLOCK), jnp.float32))
        (part_sum, hidden_grad), grad_tiles = lax.scan(
            group_step, initial,
            (shard_tiles.reshape(groups, group_size, BLOCK, BLOCK), shard_slots.reshape(groups, group_size), offsets))
        running = running + lax.optimization_barrier(part_sum.astype(jnp.bfloat16)).astype(jnp.float32)
        gate_val = gate_part.astype(jnp.float32)
        up_val = up_part.astype(jnp.float32)
        gate_sig = jax.nn.sigmoid(gate_val)
        flat_grad = hidden_grad.transpose(1, 0, 2).reshape(TOKENS, hid_width)
        gate_out = (flat_grad * up_val * gate_sig * (1.0 + gate_val * (1.0 - gate_sig))).astype(jnp.bfloat16)
        up_out = (flat_grad * (gate_val * gate_sig)).astype(jnp.bfloat16)
        return running, (grad_tiles.reshape(CAP, BLOCK, BLOCK), gate_out, up_out)

    running, (tile_grad, gate_stack, up_stack) = lax.scan(
        shard_step, jnp.zeros((MODEL_BLOCKS, TOKENS, BLOCK), jnp.float32),
        (hid_shards, weight_tiles, tile_slots, live_counts, gate_shards, up_shards))
    projected = running.transpose(1, 0, 2).reshape(TOKENS, D).astype(jnp.bfloat16)
    gate_grad = gate_stack.transpose(1, 0, 2).reshape(TOKENS, FF)
    up_grad = up_stack.transpose(1, 0, 2).reshape(TOKENS, FF)
    return projected, gate_grad, up_grad, tile_grad
```

```python
import jax
import jax.numpy as jnp
from jax import lax
from jax.experimental import pallas as pl
from jax.experimental.pallas import tpu as pltpu
from jax.sharding import PartitionSpec as P

BF = jnp.bfloat16
F32 = jnp.float32
EDGE = 128
MODEL = 32
HID = 7
RING = 8
OWN = 3
SLOTS = 96
SCALE = 4096**-0.5
COPIES = 112
DIRS = (1, -1)


def sigmoid_parts(gate, up):
    gate_val = gate.astype(F32)
    return gate_val, up.astype(F32), jax.nn.sigmoid(gate_val)


def kernel(
    gate_ref, up_ref, cot_ref, w_ref, slot_ref, live_ref,
    proj_ref, gate_out, up_out, tile_out,
    wbuf, cbuf, sbuf, sscal, invv, inv, hid, hid_t, terms, tsib, zrecv, xrecv, pbuf, yrecv, lrecv,
    ssem, rsem, lsem,
):
    d, t = lax.axis_index("dp"), lax.axis_index("tensor")
    z, xh, c = d // 4, (d // 2) % 2, d % 2
    xl, y = t // RING, t % RING
    live = live_ref[0]

    def at(pos, base):
        return lax.rem(pos + base + 2 * RING, RING)

    def on_z(step):
        return {"dp": (at(z, step) * 2 + xh) * 2 + c, "tensor": t}

    def on_y(step):
        return {"dp": d, "tensor": xl * RING + at(y, step)}

    on_x_hi = {"dp": (z * 2 + 1 - xh) * 2 + c, "tensor": t}
    on_core = {"dp": (z * 2 + xh) * 2 + 1 - c, "tensor": t}
    on_x_lo = {"dp": d, "tensor": (1 - xl) * RING + y}

    barrier = pltpu.get_barrier_semaphore()
    near = [on_z(1), on_z(-1), on_y(1), on_y(-1), on_x_hi, on_core, on_x_lo]
    for device in near:
        pl.semaphore_signal(barrier, inc=1, device_id=device, device_id_type=pl.DeviceIdType.MESH)

    copies = {}

    def send(key, src, dst, device):
        n = len(copies)
        copies[key] = pltpu.make_async_remote_copy(
            src_ref=src, dst_ref=dst, send_sem=ssem.at[n], recv_sem=rsem.at[n],
            device_id=device, device_id_type=pl.DeviceIdType.MESH,
        )
        copies[key].start()

    sent = set()

    def drain():
        for key, copy in copies.items():
            if key not in sent:
                copy.wait_send()
                sent.add(key)

    def tiles(pos, part):
        which = xh if part == 0 else 1 - xh
        return wbuf.at[pl.ds((((pos * 2) + which) * 2 + c) * OWN, OWN)]

    def last_hop(way, part):
        return 3 if part == (0 if way == 1 else 1) else 2

    def tile_send(way, k, part, src=None):
        ref = tiles(at(z, -way * k), part)
        send(("A", way, k, part), ref if src is None else src, ref, on_z(way))

    def tile_core(name, pos, part):
        ref = tiles(pos, part)
        send(("AC", name), ref, ref, on_core)

    def tile_event(k, part):
        for way in DIRS:
            if k <= last_hop(way, part):
                copies["A", way, k, part].wait_recv()
                if k + 1 <= last_hop(way, part):
                    tile_send(way, k + 1, part)
        for way in DIRS:
            if k <= last_hop(way, part):
                tile_core((way, k, part), at(z, -way * (k + 1)), part)

    def cols(pos, part):
        which = xl if part == 0 else 1 - xl
        return cbuf.at[pl.ds((which * RING + pos) * 2, 2)]

    def col_send(way, k, part):
        ref = cols(at(y, -way * k), part)
        send(("C", way, k, part), ref, ref, on_y(way))

    def col_event(k, part):
        for way in DIRS:
            if k <= last_hop(way, part):
                copies["C", way, k, part].wait_recv()
                if k + 1 <= last_hop(way, part):
                    col_send(way, k + 1, part)

    def slot_send(way, k):
        ref = sbuf.at[pl.ds(at(z, -way * k) * 4, 4)]
        send(("S", way, k), ref, ref, on_z(way))

    def slot_event(k):
        for way in DIRS:
            if k <= (3 if way == 1 else 2):
                copies["S", way, k].wait_recv()
                if k + 1 <= (3 if way == 1 else 2):
                    slot_send(way, k + 1)

    for half in range(2):
        cbuf[t * 2 + half] = cot_ref[:, half * EDGE : (half + 1) * EDGE]
    lane = lax.broadcasted_iota(jnp.int32, (1, EDGE), 1)
    sbuf[d] = jnp.where(lane == 0, slot_ref[0, 0], jnp.where(lane == 1, slot_ref[0, 1], slot_ref[0, 2]))
    pl.semaphore_wait(barrier, len(near))

    send(("S", "core"), sbuf.at[pl.ds(d, 1)], sbuf.at[pl.ds(d, 1)], on_core)
    own = w_ref.at[0]
    for way in DIRS:
        tile_send(way, 0, 0, own)
        col_send(way, 0, 0)
    send(("C", "x"), cols(y, 0), cols(y, 0), on_x_lo)
    send(("A", "x"), own, tiles(z, 0), on_x_hi)
    send(("AC", "own"), own, tiles(z, 0), on_core)
    wbuf[pl.ds(d * OWN, OWN)] = w_ref[0]
    wbuf[SLOTS] = jnp.zeros((EDGE, EDGE), BF)

    copies["S", "core"].wait_recv()
    pair = sbuf.at[pl.ds((z * 2 + xh) * 2, 2)]
    send(("S", "x"), pair, pair, on_x_hi)

    def hidden_of(h):
        piece = pl.ds(h * EDGE, EDGE) if not isinstance(h, int) else slice(h * EDGE, (h + 1) * EDGE)
        gate_val, up_val, sig = sigmoid_parts(gate_ref[:, piece], up_ref[:, piece])
        value = (gate_val * sig * up_val).astype(BF)
        hid[:, piece] = value
        hid_t[h] = value.T

    for h in range(HID):
        hidden_of(h)

    copies["C", "x"].wait_recv()
    for way in DIRS:
        col_send(way, 0, 1)
    copies["S", "x"].wait_recv()
    for way in DIRS:
        slot_send(way, 0)
    copies["A", "x"].wait_recv()
    for way in DIRS:
        tile_send(way, 0, 1)
    tile_core("x", z, 1)

    col_event(0, 0)
    tile_event(0, 0)
    col_event(0, 1)
    slot_event(0)
    tile_event(0, 1)
    col_event(1, 0)
    slot_event(1)
    col_event(1, 1)
    tile_event(1, 0)
    slot_event(2)
    col_event(2, 0)
    tile_event(1, 1)
    col_event(2, 1)
    slot_event(3)
    to_scalar = pltpu.make_async_copy(sbuf, sscal, lsem.at[0])
    to_scalar.start()
    col_event(3, 0)
    col_event(3, 1)
    to_scalar.wait()

    def quarter(q, core, add):
        def group(i, _):
            owner = (q * 4 + i) * 2 + core
            for j in range(OWN):
                slot = sscal[owner, 0, j]
                factor = jnp.where(owner * OWN + j < live, SCALE, 0.0)
                term = jnp.dot(hid_t[slot // MODEL], cbuf[lax.rem(slot, MODEL)], preferred_element_type=F32) * factor
                if add:
                    term += tsib[(q * 4 + i) * OWN + j].astype(F32)
                terms[core * 48 + (q * 4 + i) * OWN + j] = term.astype(BF)
            return 0

        lax.fori_loop(0, 4, group, 0, unroll=2)

    def for_sibling(q):
        quarter(q, 1 - c, False)
        send(
            ("T", q), terms.at[pl.ds((1 - c) * 48 + q * 12, 12)], tsib.at[pl.ds(q * 12, 12)], on_core
        )

    def for_own(q):
        copies["T", q].wait_recv()
        quarter(q, c, True)

    for_sibling(0)
    for_sibling(1)
    tile_event(2, 0)
    for_sibling(2)
    for_sibling(3)
    tile_event(2, 1)
    for_own(0)
    for_own(1)

    place = lax.broadcasted_iota(jnp.int32, (8, EDGE), 0) * EDGE + lax.broadcasted_iota(jnp.int32, (8, EDGE), 1)

    def invert(i, found):
        for j in range(OWN):
            s = i * OWN + j
            key = jnp.where(s < live, sscal[i, 0, j], -1)
            found = jnp.where(place == key, s, found)
        return found

    invv[...] = lax.fori_loop(0, SLOTS // OWN, invert, jnp.full((8, EDGE), SLOTS, jnp.int32), unroll=4)
    to_inv = pltpu.make_async_copy(invv, inv, lsem.at[1])
    to_inv.start()
    tile_event(3, 0)
    for_own(2)
    for_own(3)
    tile_event(3, 1)

    def first_hop(way, part):
        return 3 - last_hop(way, part)

    def z_local(pos, part):
        which = xh if part == 0 else 1 - xh
        return pl.ds(c * 48 + (pos * 2 + 1 - which) * OWN, OWN)

    def y_local(pos, part):
        which = xl if part == 0 else 1 - xl
        return pl.ds(((1 - which) * RING + pos) * 2, 2)

    rings = {
        "D": (terms, zrecv, z_local, z, on_z),
        "B": (pbuf, yrecv, y_local, y, on_y),
    }

    def ring_send(name, way, k, part, fresh=False):
        local, recv, index, pos, to = rings[name]
        side = 0 if way == 1 else 1
        src = local.at[index(at(pos, way * 4), part)] if k == 0 else recv.at[side, k - 1, part]
        if fresh and k:
            src = local.at[index(at(pos, way * (4 - k)), part)]
        send((name, way, k, part), src, recv.at[side, k, part], to(way))

    def ring_start(name):
        for way in DIRS:
            part = 0 if way == 1 else 1
            ring_send(name, way, 0, part, True)
        for way in DIRS:
            part = 1 if way == 1 else 0
            ring_send(name, way, 1, part, True)

    def ring_event(name, n):
        local, recv, index, pos, to = rings[name]
        for way in DIRS:
            lead = 0 if way == 1 else 1
            part = lead if n % 2 == 0 else 1 - lead
            k = (n + 1) // 2
            side = 0 if way == 1 else 1
            copies[name, way, k, part].wait_recv()
            if k < 3:
                here = index(at(pos, way * (3 - k)), part)
                recv[side, k, part] = (recv[side, k, part].astype(F32) + local[here].astype(F32)).astype(BF)
                ring_send(name, way, k + 1, part)

    def ring_total(name, part):
        local, recv, index, pos, _ = rings[name]
        return (
            recv[0, 3, part].astype(F32) + recv[1, 3, part].astype(F32) + local[index(pos, part)].astype(F32)
        )

    ring_start("D")
    for key in copies:
        if key[0] == "AC":
            copies[key].wait_recv()
    to_inv.wait()

    def weight(h, m):
        p = h * MODEL + m
        return wbuf[inv[p // EDGE, lax.rem(p, EDGE)]]

    def panel(h, m, rows):
        return jnp.concatenate(
            [jnp.concatenate([weight(h + i, m), weight(h + i, m + 1)], axis=1) for i in range(rows)], axis=0
        )

    def forward(who):
        m = who * 2
        total = jnp.dot(hid[:, 6 * EDGE :], panel(6, m, 1), preferred_element_type=F32)
        for h in (0, 2, 4):
            total += jnp.dot(hid[:, h * EDGE : (h + 2) * EDGE], panel(h, m, 2), preferred_element_type=F32)
        pbuf[m] = total[:, :EDGE].astype(BF)
        pbuf[m + 1] = total[:, EDGE:].astype(BF)

    def forward_of(step, part):
        which = xl if part == 0 else 1 - xl
        forward((1 - which) * RING + at(y, step))

    forward_of(4, 0)
    forward_of(4, 1)
    forward_of(3, 1)
    forward_of(-3, 0)
    ring_start("B")
    forward_of(3, 0)
    forward_of(-3, 1)

    def rest(i, _):
        step = jnp.where(i == 4, 0, (2 - i // 2) * (1 - 2 * lax.rem(i, 2)))
        forward_of(step, 0)
        forward_of(step, 1)
        return 0

    lax.fori_loop(0, 5, rest, 0)

    def backward(h, rows):
        def columns(i, total):
            m = i * 2
            left = jnp.concatenate([cbuf[m], cbuf[m + 1]], axis=1)
            return total + lax.dot_general(
                left, panel(h, m, rows), (((1,), (1,)), ((), ())), preferred_element_type=F32
            )

        grad = lax.fori_loop(0, MODEL // 2, columns, jnp.zeros((EDGE, rows * EDGE), F32), unroll=2)
        piece = slice(h * EDGE, (h + rows) * EDGE)
        gate_val, up_val, sig = sigmoid_parts(gate_ref[:, piece], up_ref[:, piece])
        gate_out[:, piece] = (grad * up_val * sig * (1.0 + gate_val * (1.0 - sig))).astype(BF)
        up_out[:, piece] = (grad * (gate_val * sig)).astype(BF)

    ring_event("D", 0)
    ring_event("B", 0)
    ring_event("B", 1)
    ring_event("D", 1)
    ring_event("B", 2)
    ring_event("D", 2)
    ring_event("B", 3)
    ring_event("B", 4)
    ring_event("D", 3)
    ring_event("B", 5)
    ring_event("D", 4)
    ring_event("B", 6)
    there = y_local(y, 0)
    pbuf[there] = ring_total("B", 0).astype(BF)
    send(("B", "x"), pbuf.at[there], lrecv, on_x_lo)
    backward(0, 2)
    ring_event("D", 5)
    backward(2, 2)
    copies["B", "x"].wait_recv()
    whole = ring_total("B", 1) + lrecv[...].astype(F32)
    for half in range(2):
        proj_ref[:, half * EDGE : (half + 1) * EDGE] = whole[half].astype(BF)
    ring_event("D", 6)
    there = z_local(z, 0)
    terms[there] = ring_total("D", 0).astype(BF)
    send(("D", "x"), terms.at[there], xrecv, on_x_hi)
    backward(4, 2)
    backward(6, 1)
    drain()
    copies["D", "x"].wait_recv()
    tile_out[0] = ring_total("D", 1) + xrecv[...].astype(F32)


def per_device(gate_pre, up_pre, cotangent, weight_tiles, tile_slots, live_counts):
    vmem = pl.BlockSpec(memory_space=pltpu.VMEM)
    smem = pl.BlockSpec(memory_space=pltpu.SMEM)
    tile = (EDGE, EDGE)
    return pl.pallas_call(
        kernel,
        out_shape=(
            jax.ShapeDtypeStruct(cotangent.shape, BF),
            jax.ShapeDtypeStruct(gate_pre.shape, BF),
            jax.ShapeDtypeStruct(up_pre.shape, BF),
            jax.ShapeDtypeStruct(weight_tiles.shape, F32),
        ),
        in_specs=[vmem] * 4 + [smem] * 2,
        out_specs=(vmem,) * 4,
        scratch_shapes=[
            pltpu.VMEM((SLOTS + 1, *tile), BF),
            pltpu.VMEM((MODEL, *tile), BF),
            pltpu.VMEM((SLOTS // OWN, 1, EDGE), jnp.int32),
            pltpu.SMEM((SLOTS // OWN, 1, EDGE), jnp.int32),
            pltpu.VMEM((8, EDGE), jnp.int32),
            pltpu.SMEM((8, EDGE), jnp.int32),
            pltpu.VMEM((EDGE, HID * EDGE), BF),
            pltpu.VMEM((HID, *tile), BF),
            pltpu.VMEM((SLOTS, *tile), BF),
            pltpu.VMEM((SLOTS // 2, *tile), BF),
            pltpu.VMEM((2, 4, 2, OWN, *tile), BF),
            pltpu.VMEM((OWN, *tile), BF),
            pltpu.VMEM((MODEL, *tile), BF),
            pltpu.VMEM((2, 4, 2, 2, *tile), BF),
            pltpu.VMEM((2, *tile), BF),
            pltpu.SemaphoreType.DMA((COPIES,)),
            pltpu.SemaphoreType.DMA((COPIES,)),
            pltpu.SemaphoreType.DMA((2,)),
        ],
        compiler_params=pltpu.CompilerParams(
            collective_id=0, has_side_effects=True, vmem_limit_bytes=40 << 20
        ),
    )(gate_pre, up_pre, cotangent, weight_tiles, tile_slots, live_counts)


def solution(mesh):
    in_specs = (
        P("dp", "tensor"),
        P("dp", "tensor"),
        P("dp", "tensor"),
        P("tensor", "dp", None, None),
        P("tensor", "dp"),
        P("tensor"),
    )
    out_specs = (
        P("dp", "tensor"),
        P("dp", "tensor"),
        P("dp", "tensor"),
        P("tensor", "dp", None, None),
    )
    return jax.shard_map(
        per_device, mesh=mesh, in_specs=in_specs, out_specs=out_specs, check_vma=False
    )
```

```python
import math

import jax
import jax.numpy as jnp
from jax import lax
from jax.experimental import pallas as pl
from jax.experimental.pallas import tpu as pltpu
from jax.sharding import PartitionSpec as P

BF = jnp.bfloat16
F32 = jnp.float32
EDGE = 128
MODEL = 32
HID = 7
RING = 8
OWN = 3
SLOTS = 96
SCALE = 4096**-0.5
DIRS = (1, -1)
FAR_FIRST = (4, 3, 5, 2, 6, 1, 7, 0)
VMEM_BYTES = 62 << 20
SEND_SEMS, RECV_SEMS = 7, 84


def sigmoid_parts(gate, up):
    gate_val = gate.astype(F32)
    return gate_val, up.astype(F32), jax.nn.sigmoid(gate_val)


class Traffic:
    def __init__(self, send_sems, recv_sems):
        self.send_sems, self.recv_sems = send_sems, recv_sems
        self.leaving, self.coming = {}, {}
        self.ids = {}

    def sem(self, sems, kind, key):
        ids = self.ids.setdefault(kind, {})
        return sems.at[ids.setdefault(key, len(ids))]

    def send(self, family, key, src, dst, device):
        copy = pltpu.make_async_remote_copy(
            src_ref=src,
            dst_ref=dst,
            send_sem=self.sem(self.send_sems, "leave", family),
            recv_sem=self.sem(self.recv_sems, "come", (family, key)),
            device_id=device,
            device_id_type=pl.DeviceIdType.MESH,
        )
        copy.start()
        self.leaving.setdefault(family, []).append((copy, math.prod(src.shape)))
        self.coming.setdefault((family, key), []).append((copy, math.prod(dst.shape), device))

    def arrive(self, family, key, like):
        copies = self.coming.pop((family, key))
        assert sum(c[1] for c in copies) == math.prod(like.shape)
        sem = self.sem(self.recv_sems, "come", (family, key))
        pltpu.make_async_remote_copy(
            src_ref=like, dst_ref=like, send_sem=sem, recv_sem=sem,
            device_id=copies[0][2], device_id_type=pl.DeviceIdType.MESH,
        ).wait_recv()

    def left(self, family, like):
        copies = self.leaving.pop(family)
        assert sum(c[1] for c in copies) == math.prod(like.shape)
        sem = self.sem(self.send_sems, "leave", family)
        pltpu.make_async_remote_copy(
            src_ref=like, dst_ref=like, send_sem=sem, recv_sem=sem,
            device_id=self.coming_device, device_id_type=pl.DeviceIdType.MESH,
        ).wait_send()


def kernel(
    gate_hbm, up_hbm, cot_hbm, w_hbm, slot_ref, live_ref,
    proj_hbm, gate_out_hbm, up_out_hbm, tile_hbm,
    proj_ref, gate_out, up_out, tile_out, gate_ref, up_ref, wbuf, cbuf, sbuf, sscal, invv, inv, hid, hid_t, terms, tsib, zrecv, xrecv, pbuf, yrecv, lrecv,
    ssem, rsem, lsem,
):
    d, t = lax.axis_index("dp"), lax.axis_index("tensor")
    z, xh, c = d // 4, (d // 2) % 2, d % 2
    xl, y = t // RING, t % RING

    def at(pos, base):
        return lax.rem(pos + base + 2 * RING, RING)

    def on_z(step):
        return {"dp": (at(z, step) * 2 + xh) * 2 + c, "tensor": t}

    def on_y(step):
        return {"dp": d, "tensor": xl * RING + at(y, step)}

    on_x_hi = {"dp": (z * 2 + 1 - xh) * 2 + c, "tensor": t}
    on_core = {"dp": (z * 2 + xh) * 2 + 1 - c, "tensor": t}
    on_x_lo = {"dp": d, "tensor": (1 - xl) * RING + y}

    loads = [
        pltpu.make_async_copy(w_hbm.at[0], wbuf.at[pl.ds(d * OWN, OWN)], lsem.at[0]),
        pltpu.make_async_copy(cot_hbm.at[:, pl.ds(0, EDGE)], cbuf.at[t * 2], lsem.at[1]),
        pltpu.make_async_copy(cot_hbm.at[:, pl.ds(EDGE, EDGE)], cbuf.at[t * 2 + 1], lsem.at[2]),
        pltpu.make_async_copy(gate_hbm, gate_ref, lsem.at[3]),
        pltpu.make_async_copy(up_hbm, up_ref, lsem.at[4]),
    ]
    for load in loads:
        load.start()

    barrier = pltpu.get_barrier_semaphore()
    near = [on_z(i) for i in range(1, RING)] + [on_y(1), on_y(-1), on_x_hi, on_core, on_x_lo]
    for device in near:
        pl.semaphore_signal(barrier, inc=1, device_id=device, device_id_type=pl.DeviceIdType.MESH)

    live = live_ref[0]
    traffic = Traffic(ssem, rsem)
    traffic.coming_device = on_core

    def tiles(pos, part, first=0, count=OWN):
        which = xh if part == 0 else 1 - xh
        return wbuf.at[pl.ds((((pos * 2) + which) * 2 + c) * OWN + first, count)]

    def last_hop(way, part):
        return 3 if part == (0 if way == 1 else 1) else 2

    def ways_of(k, part):
        return [way for way in DIRS if k <= last_hop(way, part)]

    def tile_send(way, k, part, i):
        ref = tiles(at(z, -way * k), part, i, 1)
        traffic.send("A", (k, part, i), ref, ref, on_z(way))

    def tile_core(pos, part):
        ref = tiles(pos, part)
        traffic.send("K", 0, ref, ref, on_core)

    def tile_event(k, part, i):
        ways = ways_of(k, part)
        traffic.arrive("A", (k, part, i), wbuf.at[pl.ds(0, len(ways))])
        for way in ways_of(k + 1, part):
            tile_send(way, k + 1, part, i)
        if i == OWN - 1:
            for way in ways:
                tile_core(at(z, -way * (k + 1)), part)

    def tile_x_event(i):
        traffic.arrive("A", ("x", i), wbuf.at[pl.ds(0, 1)])
        for way in DIRS:
            tile_send(way, 0, 1, i)
        if i == OWN - 1:
            tile_core(z, 1)

    def column(pos, part, i):
        which = xl if part == 0 else 1 - xl
        return cbuf.at[pl.ds((which * RING + pos) * 2 + i, 1)]

    def col_send(way, k, part, i):
        ref = column(at(y, -way * k), part, i)
        traffic.send("C", (k, part, i), ref, ref, on_y(way))

    def col_event(k, part, i):
        traffic.arrive("C", (k, part, i), cbuf.at[pl.ds(0, len(ways_of(k, part)))])
        for way in ways_of(k + 1, part):
            col_send(way, k + 1, part, i)

    def col_x_event(i):
        traffic.arrive("C", ("x", i), cbuf.at[pl.ds(0, 1)])
        for way in DIRS:
            col_send(way, 0, 1, i)

    def rows(first, count):
        return sbuf.at[pl.ds(first, count)]

    def row_z_event():
        traffic.arrive("S", "z", rows(0, RING - 1))
        ref = rows((c * 2 + xh) * RING, RING)
        traffic.send("S", "x", ref, ref, on_x_hi)

    def row_x_event():
        traffic.arrive("S", "x", rows(0, RING))
        ref = rows(c * 2 * RING, 2 * RING)
        traffic.send("S", "core", ref, ref, on_core)

    lane = lax.broadcasted_iota(jnp.int32, (1, EDGE), 1)
    mine = (c * 2 + xh) * RING + z
    sbuf[mine] = jnp.where(lane == 0, slot_ref[0, 0], jnp.where(lane == 1, slot_ref[0, 1], slot_ref[0, 2]))
    wbuf[SLOTS] = jnp.zeros((EDGE, EDGE), BF)
    loads[0].wait()
    pl.semaphore_wait(barrier, len(near))

    for i in range(1, RING):
        traffic.send("S", "z", rows(mine, 1), rows(mine, 1), on_z(i))
    for i in range(OWN):
        ref = tiles(z, 0, i, 1)
        traffic.send("A", ("x", i), ref, ref, on_x_hi)
        for way in DIRS:
            tile_send(way, 0, 0, i)
    loads[1].wait()
    loads[2].wait()
    for i in range(2):
        ref = column(y, 0, i)
        traffic.send("C", ("x", i), ref, ref, on_x_lo)
        for way in DIRS:
            col_send(way, 0, 0, i)
    tile_core(z, 0)
    loads[3].wait()
    loads[4].wait()

    def hidden_of(h):
        piece = slice(h * EDGE, (h + 1) * EDGE)
        gate_val, up_val, sig = sigmoid_parts(gate_ref[:, piece], up_ref[:, piece])
        value = (gate_val * sig * up_val).astype(BF)
        hid[:, piece] = value
        hid_t[h] = value.T

    for h in range(HID):
        hidden_of(h)

    tile_event(0, 0, 0)
    col_event(0, 0, 0)
    col_x_event(0)
    tile_event(0, 0, 1)
    col_event(0, 0, 1)
    col_x_event(1)
    tile_x_event(0)
    tile_event(0, 0, 2)
    row_z_event()
    tile_x_event(1)
    tile_x_event(2)
    tile_event(1, 0, 0)
    col_event(1, 0, 0)
    col_event(0, 1, 0)
    tile_event(1, 0, 1)
    col_event(1, 0, 1)
    tile_event(0, 1, 0)
    row_x_event()
    col_event(0, 1, 1)
    tile_event(1, 0, 2)
    tile_event(0, 1, 1)
    col_event(2, 0, 0)
    tile_event(0, 1, 2)
    col_event(1, 1, 0)
    traffic.arrive("S", "core", rows(0, 2 * RING))
    to_scalar = pltpu.make_async_copy(sbuf, sscal, lsem.at[0])
    to_scalar.start()
    col_event(2, 0, 1)
    tile_event(2, 0, 0)
    col_event(1, 1, 1)
    tile_event(2, 0, 1)
    col_event(3, 0, 0)
    tile_event(1, 1, 0)
    col_event(2, 1, 0)
    tile_event(2, 0, 2)
    to_scalar.wait()

    def row_of(owner_z, owner_x, owner_core):
        return (owner_core * 2 + owner_x) * RING + owner_z

    place = lax.broadcasted_iota(jnp.int32, (8, EDGE), 0) * EDGE + lax.broadcasted_iota(jnp.int32, (8, EDGE), 1)

    def invert(i, found):
        row = row_of(i // 4, lax.rem(i // 2, 2), lax.rem(i, 2))
        for j in range(OWN):
            s = i * OWN + j
            key = jnp.where(s < live, sscal[row, 0, j], -1)
            found = jnp.where(place == key, s, found)
        return found

    invv[...] = lax.fori_loop(0, SLOTS // OWN, invert, jnp.full((8, EDGE), SLOTS, jnp.int32), unroll=4)
    to_inv = pltpu.make_async_copy(invv, inv, lsem.at[1])
    to_inv.start()

    col_event(3, 0, 1)
    tile_event(1, 1, 1)
    col_event(2, 1, 1)
    tile_event(1, 1, 2)
    tile_event(3, 0, 0)
    col_event(3, 1, 0)
    col_event(3, 1, 1)

    def group(owner_z, core, add):
        for owner_x in range(2):
            row = row_of(owner_z, owner_x, core)
            for j in range(OWN):
                slot = sscal[row, 0, j]
                s = ((owner_z * 2 + owner_x) * 2 + core) * OWN + j
                factor = jnp.where(s < live, SCALE, 0.0)
                term = jnp.dot(hid_t[slot // MODEL], cbuf[lax.rem(slot, MODEL)], preferred_element_type=F32) * factor
                index = (owner_z * 2 + owner_x) * OWN + j
                if add:
                    term += tsib[index].astype(F32)
                terms[core * 48 + index] = term.astype(BF)

    def for_sibling(n):
        owner_z = at(z, FAR_FIRST[n])
        group(owner_z, 1 - c, False)
        traffic.send(
            "T", n, terms.at[pl.ds((1 - c) * 48 + owner_z * 6, 6)], tsib.at[pl.ds(owner_z * 6, 6)], on_core
        )

    def for_own(n):
        traffic.arrive("T", n, tsib.at[pl.ds(0, 6)])
        group(at(z, FAR_FIRST[n]), c, True)

    def z_local(pos, part):
        which = 1 - xh if part == 0 else xh
        return pl.ds(c * 48 + (pos * 2 + which) * OWN, OWN)

    def y_local(pos, part, i):
        which = 1 - xl if part == 0 else xl
        return pl.ds((which * RING + pos) * 2 + i, 1)

    def y_fresh(way, k, part):
        side = 0 if way == 1 else 1
        for i in range(2):
            src = pbuf.at[y_local(at(y, way * (4 - k)), part, i)]
            traffic.send("B", (k, part if way == 1 else 1 - part, i), src, yrecv.at[side, k, part, pl.ds(i, 1)], on_y(way))

    def z_key(way, k, part):
        return (k, part if way == 1 else 1 - part)

    def z_start():
        for k in range(2):
            for way in DIRS:
                part = k if way == 1 else 1 - k
                src = terms.at[z_local(at(z, way * (4 - k)), part)]
                side = 0 if way == 1 else 1
                traffic.send("D", z_key(way, k, part), src, zrecv.at[side, k, part], on_z(way))

    def z_event(n):
        k, lead = (n + 1) // 2, n % 2
        traffic.arrive("D", (k, lead), terms.at[pl.ds(0, 2 * OWN)])
        for way in DIRS:
            part = lead if way == 1 else 1 - lead
            side = 0 if way == 1 else 1
            if k < 3:
                here = z_local(at(z, way * (3 - k)), part)
                zrecv[side, k, part] = (zrecv[side, k, part].astype(F32) + terms[here].astype(F32)).astype(BF)
                traffic.send(
                    "D", z_key(way, k + 1, part), zrecv.at[side, k, part], zrecv.at[side, k + 1, part], on_z(way)
                )

    def z_total(part):
        return (
            zrecv[0, 3, part].astype(F32) + zrecv[1, 3, part].astype(F32) + terms[z_local(z, part)].astype(F32)
        )

    def y_start(k):
        for way in DIRS:
            y_fresh(way, k, k if way == 1 else 1 - k)

    def y_event(n, i):
        k, lead = (n + 1) // 2, n % 2
        traffic.arrive("B", (k, lead, i), pbuf.at[pl.ds(0, 2)])
        for way in DIRS:
            part = lead if way == 1 else 1 - lead
            side = 0 if way == 1 else 1
            if k < 3:
                here = y_local(at(y, way * (3 - k)), part, i)
                held = yrecv.at[side, k, part, pl.ds(i, 1)]
                held[...] = (held[...].astype(F32) + pbuf[here].astype(F32)).astype(BF)
                traffic.send("B", (k + 1, lead, i), held, yrecv.at[side, k + 1, part, pl.ds(i, 1)], on_y(way))

    def y_total(part, i):
        return (
            yrecv[0, 3, part, i].astype(F32) + yrecv[1, 3, part, i].astype(F32)
            + pbuf[y_local(y, part, i)][0].astype(F32)
        )

    for_sibling(0)
    for_sibling(1)
    for_sibling(2)
    tile_event(3, 0, 1)
    tile_event(2, 1, 0)
    for_own(0)
    for_own(1)
    for_own(2)
    tile_event(3, 0, 2)
    tile_event(2, 1, 1)
    tile_event(2, 1, 2)
    z_start()
    for n in range(3, 8):
        for_sibling(n)
    tile_event(3, 1, 0)
    tile_event(3, 1, 1)
    tile_event(3, 1, 2)
    for n in range(3, 6):
        for_own(n)
    to_inv.wait()
    traffic.arrive("K", 0, wbuf.at[pl.ds(0, 48)])

    def weight(h, m):
        p = h * MODEL + m
        return wbuf[inv[p // EDGE, lax.rem(p, EDGE)]]

    def panel(h, m, count):
        return jnp.concatenate(
            [jnp.concatenate([weight(h + i, m), weight(h + i, m + 1)], axis=1) for i in range(count)], axis=0
        )

    def forward_of(step, part):
        which = 1 - xl if part == 0 else xl
        m = (which * RING + at(y, step)) * 2
        total = jnp.dot(hid[:, 6 * EDGE :], panel(6, m, 1), preferred_element_type=F32)
        for h in (0, 2, 4):
            total += jnp.dot(hid[:, h * EDGE : (h + 2) * EDGE], panel(h, m, 2), preferred_element_type=F32)
        pbuf[m] = total[:, :EDGE].astype(BF)
        pbuf[m + 1] = total[:, EDGE:].astype(BF)

    def backward(h, count):
        def columns(i, total):
            m = i * 2
            left = jnp.concatenate([cbuf[m], cbuf[m + 1]], axis=1)
            return total + lax.dot_general(
                left, panel(h, m, count), (((1,), (1,)), ((), ())), preferred_element_type=F32
            )

        grad = lax.fori_loop(0, MODEL // 2, columns, jnp.zeros((EDGE, count * EDGE), F32), unroll=2)
        piece = slice(h * EDGE, (h + count) * EDGE)
        gate_val, up_val, sig = sigmoid_parts(gate_ref[:, piece], up_ref[:, piece])
        gate_out[:, piece] = (grad * up_val * sig * (1.0 + gate_val * (1.0 - sig))).astype(BF)
        up_out[:, piece] = (grad * (gate_val * sig)).astype(BF)

    forward_of(4, 0)
    forward_of(4, 1)
    y_start(0)
    forward_of(3, 1)
    forward_of(-3, 0)
    y_start(1)
    z_event(0)
    for_own(6)
    for_own(7)
    forward_of(3, 0)
    forward_of(-3, 1)

    def rest(i, _):
        step = (2 - i // 2) * (1 - 2 * lax.rem(i, 2))
        forward_of(step, 0)
        forward_of(step, 1)
        return 0

    lax.fori_loop(0, 4, rest, 0)
    z_event(1)
    y_event(0, 0)
    y_event(0, 1)
    y_event(1, 0)
    y_event(1, 1)
    forward_of(0, 0)
    forward_of(0, 1)
    z_event(2)
    y_event(2, 0)
    y_event(2, 1)
    y_event(3, 0)
    z_event(3)
    y_event(3, 1)
    y_event(4, 0)
    y_event(4, 1)
    z_event(4)
    y_event(5, 0)
    y_event(5, 1)
    backward(0, 2)
    z_event(5)
    for i in range(2):
        y_event(6, i)
        there = y_local(y, 0, i)
        pbuf[there] = y_total(0, i).astype(BF)[None]
        traffic.send("B", ("x", i), pbuf.at[there], lrecv.at[pl.ds(i, 1)], on_x_lo)
    backward(2, 2)
    z_event(6)
    there = z_local(z, 0)
    terms[there] = z_total(0).astype(BF)
    traffic.send("D", "x", terms.at[there], xrecv, on_x_hi)
    backward(4, 2)
    backward(6, 1)
    for i in range(2):
        traffic.arrive("B", ("x", i), lrecv.at[pl.ds(0, 1)])
        proj_ref[:, i * EDGE : (i + 1) * EDGE] = (y_total(1, i) + lrecv[i].astype(F32)).astype(BF)
    stores = [
        pltpu.make_async_copy(gate_out, gate_out_hbm, lsem.at[0]),
        pltpu.make_async_copy(up_out, up_out_hbm, lsem.at[1]),
        pltpu.make_async_copy(proj_ref, proj_hbm, lsem.at[2]),
        pltpu.make_async_copy(tile_out, tile_hbm, lsem.at[3]),
    ]
    for store in stores[:3]:
        store.start()
    traffic.left("S", rows(0, 7 + 8 + 16))
    traffic.left("A", wbuf.at[pl.ds(0, 45)])
    traffic.left("K", wbuf.at[pl.ds(0, 48)])
    traffic.left("C", cbuf.at[pl.ds(0, 30)])
    traffic.left("T", tsib.at[pl.ds(0, 48)])
    traffic.left("B", pbuf.at[pl.ds(0, 30)])
    traffic.arrive("D", "x", xrecv)
    tile_out[0] = z_total(1) + xrecv[...].astype(F32)
    stores[3].start()
    traffic.left("D", terms.at[pl.ds(0, 45)])
    for store in stores:
        store.wait()


def hand_out(*refs):
    n = (len(refs) - 1) // 3
    given, out, held, sems = refs[:n], refs[n : 2 * n], refs[2 * n : 3 * n], refs[-1]
    loads = [pltpu.make_async_copy(given[i], held[i], sems.at[0, i]) for i in range(n)]
    stores = [pltpu.make_async_copy(held[i], out[i], sems.at[1, i]) for i in range(n)]
    for load in loads:
        load.start()
    for load, store in zip(loads, stores):
        load.wait()
        store.start()
    for store in stores:
        store.wait()


def per_device(gate_pre, up_pre, cotangent, weight_tiles, tile_slots, live_counts):
    smem = pl.BlockSpec(memory_space=pltpu.SMEM)
    hbm = pl.BlockSpec(memory_space=pl.ANY)
    tile = (EDGE, EDGE)
    shapes = (
        jax.ShapeDtypeStruct(cotangent.shape, BF),
        jax.ShapeDtypeStruct(gate_pre.shape, BF),
        jax.ShapeDtypeStruct(up_pre.shape, BF),
        jax.ShapeDtypeStruct(weight_tiles.shape, F32),
    )
    results = pl.pallas_call(
        kernel,
        out_shape=shapes,
        in_specs=[hbm] * 4 + [smem] * 2,
        out_specs=(hbm,) * 4,
        scratch_shapes=[
            *[pltpu.VMEM(shape.shape, shape.dtype) for shape in shapes],
            pltpu.VMEM(gate_pre.shape, BF),
            pltpu.VMEM(up_pre.shape, BF),
            pltpu.VMEM((SLOTS + 1, *tile), BF),
            pltpu.VMEM((MODEL, *tile), BF),
            pltpu.VMEM((SLOTS // OWN, 1, EDGE), jnp.int32),
            pltpu.SMEM((SLOTS // OWN, 1, EDGE), jnp.int32),
            pltpu.VMEM((8, EDGE), jnp.int32),
            pltpu.SMEM((8, EDGE), jnp.int32),
            pltpu.VMEM((EDGE, HID * EDGE), BF),
            pltpu.VMEM((HID, *tile), BF),
            pltpu.VMEM((SLOTS, *tile), BF),
            pltpu.VMEM((SLOTS // 2, *tile), BF),
            pltpu.VMEM((2, 4, 2, OWN, *tile), BF),
            pltpu.VMEM((OWN, *tile), BF),
            pltpu.VMEM((MODEL, *tile), BF),
            pltpu.VMEM((2, 4, 2, 2, *tile), BF),
            pltpu.VMEM((2, *tile), BF),
            pltpu.SemaphoreType.DMA((SEND_SEMS,)),
            pltpu.SemaphoreType.DMA((RECV_SEMS,)),
            pltpu.SemaphoreType.DMA((5,)),
        ],
        compiler_params=pltpu.CompilerParams(
            collective_id=0, has_side_effects=True, vmem_limit_bytes=VMEM_BYTES
        ),
    )(gate_pre, up_pre, cotangent, weight_tiles, tile_slots, live_counts)
    return pl.pallas_call(
        hand_out,
        out_shape=shapes,
        in_specs=[hbm] * 4,
        out_specs=(hbm,) * 4,
        scratch_shapes=[pltpu.VMEM(shape.shape, shape.dtype) for shape in shapes] + [pltpu.SemaphoreType.DMA((2, 4))],
        compiler_params=pltpu.CompilerParams(vmem_limit_bytes=VMEM_BYTES),
    )(*results)


def solution(mesh):
    in_specs = (
        P("dp", "tensor"),
        P("dp", "tensor"),
        P("dp", "tensor"),
        P("tensor", "dp", None, None),
        P("tensor", "dp"),
        P("tensor"),
    )
    out_specs = (
        P("dp", "tensor"),
        P("dp", "tensor"),
        P("dp", "tensor"),
        P("tensor", "dp", None, None),
    )
    return jax.shard_map(
        per_device, mesh=mesh, in_specs=in_specs, out_specs=out_specs, check_vma=False
    )
```

```python
import math

import jax
import jax.numpy as jnp
from jax import lax
from jax.experimental import pallas as pl
from jax.experimental.pallas import tpu as pltpu
from jax.sharding import PartitionSpec as P

BF = jnp.bfloat16
F32 = jnp.float32
EDGE = 128
MODEL = 32
HID = 7
RING = 8
OWN = 3
SLOTS = 96
SCALE = 4096**-0.5
DIRS = (1, -1)
FAR_FIRST = (4, 3, 5, 2, 6, 1, 7, 0)
VMEM_BYTES = 62 << 20
SEND_SEMS, RECV_SEMS = 7, 112


def sigmoid_parts(gate, up):
    gate_val = gate.astype(F32)
    return gate_val, up.astype(F32), jax.nn.sigmoid(gate_val)


class Traffic:
    def __init__(self, send_sems, recv_sems):
        self.send_sems, self.recv_sems = send_sems, recv_sems
        self.leaving, self.coming = {}, {}
        self.ids = {}

    def sem(self, sems, kind, key):
        ids = self.ids.setdefault(kind, {})
        return sems.at[ids.setdefault(key, len(ids))]

    def send(self, family, key, src, dst, device):
        copy = pltpu.make_async_remote_copy(
            src_ref=src,
            dst_ref=dst,
            send_sem=self.sem(self.send_sems, "leave", family),
            recv_sem=self.sem(self.recv_sems, "come", (family, key)),
            device_id=device,
            device_id_type=pl.DeviceIdType.MESH,
        )
        copy.start()
        self.leaving.setdefault(family, []).append((copy, math.prod(src.shape)))
        self.coming.setdefault((family, key), []).append((copy, math.prod(dst.shape), device))

    def arrive(self, family, key, like):
        copies = self.coming.pop((family, key))
        assert sum(c[1] for c in copies) == math.prod(like.shape)
        sem = self.sem(self.recv_sems, "come", (family, key))
        pltpu.make_async_remote_copy(
            src_ref=like, dst_ref=like, send_sem=sem, recv_sem=sem,
            device_id=copies[0][2], device_id_type=pl.DeviceIdType.MESH,
        ).wait_recv()

    def left(self, family, like):
        copies = self.leaving.pop(family)
        assert sum(c[1] for c in copies) == math.prod(like.shape)
        sem = self.sem(self.send_sems, "leave", family)
        pltpu.make_async_remote_copy(
            src_ref=like, dst_ref=like, send_sem=sem, recv_sem=sem,
            device_id=self.coming_device, device_id_type=pl.DeviceIdType.MESH,
        ).wait_send()


def kernel(
    gate_hbm, up_hbm, cot_hbm, w_hbm, slot_ref, live_ref,
    proj_hbm, gate_out_hbm, up_out_hbm, tile_hbm,
    proj_ref, gate_out, up_out, tile_out, gate_ref, up_ref, wbuf, cbuf, sbuf, sscal, invv, inv, hid, hid_t, terms, tsib, zrecv, xrecv, pbuf, yrecv, lrecv, zfirst, yfirst,
    ssem, rsem, lsem,
):
    d, t = lax.axis_index("dp"), lax.axis_index("tensor")
    z, xh, c = d // 4, (d // 2) % 2, d % 2
    xl, y = t // RING, t % RING

    def at(pos, base):
        return lax.rem(pos + base + 2 * RING, RING)

    def on_z(step):
        return {"dp": (at(z, step) * 2 + xh) * 2 + c, "tensor": t}

    def on_y(step):
        return {"dp": d, "tensor": xl * RING + at(y, step)}

    on_x_hi = {"dp": (z * 2 + 1 - xh) * 2 + c, "tensor": t}
    on_core = {"dp": (z * 2 + xh) * 2 + 1 - c, "tensor": t}
    on_x_lo = {"dp": d, "tensor": (1 - xl) * RING + y}

    loads = [
        pltpu.make_async_copy(w_hbm.at[0], wbuf.at[pl.ds(d * OWN, OWN)], lsem.at[0]),
        pltpu.make_async_copy(cot_hbm.at[:, pl.ds(0, EDGE)], cbuf.at[t * 2], lsem.at[1]),
        pltpu.make_async_copy(cot_hbm.at[:, pl.ds(EDGE, EDGE)], cbuf.at[t * 2 + 1], lsem.at[2]),
        pltpu.make_async_copy(gate_hbm, gate_ref, lsem.at[3]),
        pltpu.make_async_copy(up_hbm, up_ref, lsem.at[4]),
    ]
    for load in loads:
        load.start()

    barrier = pltpu.get_barrier_semaphore()
    near = [on_z(i) for i in range(1, RING)] + [on_y(1), on_y(-1), on_x_hi, on_core, on_x_lo]
    for device in near:
        pl.semaphore_signal(barrier, inc=1, device_id=device, device_id_type=pl.DeviceIdType.MESH)

    live = live_ref[0]
    traffic = Traffic(ssem, rsem)
    traffic.coming_device = on_core

    def tiles(pos, part, first=0, count=OWN):
        which = xh if part == 0 else 1 - xh
        return wbuf.at[pl.ds((((pos * 2) + which) * 2 + c) * OWN + first, count)]

    def gather_ways(count, k, part, i):
        if part == 1:
            return DIRS if k < 3 else ()
        return DIRS if k < 3 else (half_way(count, i),) if k == 3 else ()

    def half_way(count, i):
        return 1 if i < (count + 1) // 2 else -1

    def tile_send(way, k, part, i):
        ref = tiles(at(z, -way * k), part, i, 1)
        traffic.send("A", (k, part, i), ref, ref, on_z(way))

    def tile_core(pos, part):
        ref = tiles(pos, part)
        traffic.send("K", 0, ref, ref, on_core)

    def tile_cores(k, part):
        for way in DIRS if k < 3 else (1,):
            tile_core(at(z, -way * (k + 1)), part)

    def tile_event(k, part, i):
        ways = gather_ways(OWN, k, part, i)
        traffic.arrive("A", (k, part, i), wbuf.at[pl.ds(0, len(ways))])
        for way in gather_ways(OWN, k + 1, part, i):
            tile_send(way, k + 1, part, i)
        if part == 0 and k == 3:
            for way in ways:
                ref = tiles(at(z, -way * (k + 1)), 0, i, 1)
                traffic.send("A", ("far", i), ref, ref, on_x_hi)
        if i == OWN - 1:
            tile_cores(k, part)

    def tile_far_event(i):
        traffic.arrive("A", ("far", i), wbuf.at[pl.ds(0, 1)])
        if i == OWN - 1:
            tile_cores(3, 1)

    def tile_x_event(i):
        traffic.arrive("A", ("x", i), wbuf.at[pl.ds(0, 1)])
        for way in DIRS:
            tile_send(way, 0, 1, i)
        if i == OWN - 1:
            tile_core(z, 1)

    def column(pos, part, i):
        which = xl if part == 0 else 1 - xl
        return cbuf.at[pl.ds((which * RING + pos) * 2 + i, 1)]

    def col_send(way, k, part, i):
        ref = column(at(y, -way * k), part, i)
        traffic.send("C", (k, part, i), ref, ref, on_y(way))

    def col_event(k, part, i):
        ways = gather_ways(2, k, part, i)
        traffic.arrive("C", (k, part, i), cbuf.at[pl.ds(0, len(ways))])
        for way in gather_ways(2, k + 1, part, i):
            col_send(way, k + 1, part, i)
        if part == 0 and k == 3:
            for way in ways:
                ref = column(at(y, -way * (k + 1)), 0, i)
                traffic.send("C", ("far", i), ref, ref, on_x_lo)

    def col_far_event(i):
        traffic.arrive("C", ("far", i), cbuf.at[pl.ds(0, 1)])

    def col_x_event(i):
        traffic.arrive("C", ("x", i), cbuf.at[pl.ds(0, 1)])
        for way in DIRS:
            col_send(way, 0, 1, i)

    def rows(first, count):
        return sbuf.at[pl.ds(first, count)]

    def row_z_event():
        traffic.arrive("S", "z", rows(0, RING - 1))
        ref = rows((c * 2 + xh) * RING, RING)
        traffic.send("S", "x", ref, ref, on_x_hi)

    def row_x_event():
        traffic.arrive("S", "x", rows(0, RING))
        ref = rows(c * 2 * RING, 2 * RING)
        traffic.send("S", "core", ref, ref, on_core)

    lane = lax.broadcasted_iota(jnp.int32, (1, EDGE), 1)
    mine = (c * 2 + xh) * RING + z
    sbuf[mine] = jnp.where(lane == 0, slot_ref[0, 0], jnp.where(lane == 1, slot_ref[0, 1], slot_ref[0, 2]))
    wbuf[SLOTS] = jnp.zeros((EDGE, EDGE), BF)
    loads[0].wait()
    pl.semaphore_wait(barrier, len(near))

    for i in range(1, RING):
        traffic.send("S", "z", rows(mine, 1), rows(mine, 1), on_z(i))
    for i in range(OWN):
        ref = tiles(z, 0, i, 1)
        traffic.send("A", ("x", i), ref, ref, on_x_hi)
        for way in DIRS:
            tile_send(way, 0, 0, i)
    loads[1].wait()
    loads[2].wait()
    for i in range(2):
        ref = column(y, 0, i)
        traffic.send("C", ("x", i), ref, ref, on_x_lo)
        for way in DIRS:
            col_send(way, 0, 0, i)
    tile_core(z, 0)
    loads[3].wait()
    loads[4].wait()

    def hidden_of(h):
        piece = slice(h * EDGE, (h + 1) * EDGE)
        gate_val, up_val, sig = sigmoid_parts(gate_ref[:, piece], up_ref[:, piece])
        value = (gate_val * sig * up_val).astype(BF)
        hid[:, piece] = value
        hid_t[h] = value.T

    for h in range(HID):
        hidden_of(h)

    tile_event(0, 0, 0)
    col_event(0, 0, 0)
    row_z_event()
    col_x_event(0)
    tile_event(0, 0, 1)
    tile_x_event(0)
    col_event(0, 0, 1)
    col_x_event(1)
    tile_event(0, 0, 2)
    tile_x_event(1)
    tile_x_event(2)
    tile_event(1, 0, 0)
    col_event(1, 0, 0)
    row_x_event()
    tile_event(1, 0, 1)
    col_event(0, 1, 0)
    tile_event(0, 1, 0)
    col_event(1, 0, 1)
    traffic.arrive("S", "core", rows(0, 2 * RING))
    to_scalar = pltpu.make_async_copy(sbuf, sscal, lsem.at[0])
    to_scalar.start()
    tile_event(1, 0, 2)
    col_event(0, 1, 1)
    tile_event(0, 1, 1)
    tile_event(0, 1, 2)
    col_event(2, 0, 0)
    col_event(1, 1, 0)
    tile_event(2, 0, 0)
    col_event(2, 0, 1)
    tile_event(2, 0, 1)
    tile_event(1, 1, 0)
    col_event(1, 1, 1)
    tile_event(2, 0, 2)
    to_scalar.wait()

    def row_of(owner_z, owner_x, owner_core):
        return (owner_core * 2 + owner_x) * RING + owner_z

    place = lax.broadcasted_iota(jnp.int32, (8, EDGE), 0) * EDGE + lax.broadcasted_iota(jnp.int32, (8, EDGE), 1)

    def invert(i, found):
        row = row_of(i // 4, lax.rem(i // 2, 2), lax.rem(i, 2))
        for j in range(OWN):
            s = i * OWN + j
            key = jnp.where(s < live, sscal[row, 0, j], -1)
            found = jnp.where(place == key, s, found)
        return found

    invv[...] = lax.fori_loop(0, SLOTS // OWN, invert, jnp.full((8, EDGE), SLOTS, jnp.int32), unroll=4)
    to_inv = pltpu.make_async_copy(invv, inv, lsem.at[1])
    to_inv.start()

    col_event(3, 0, 0)
    tile_event(1, 1, 1)
    col_event(2, 1, 0)
    tile_event(1, 1, 2)
    col_event(3, 0, 1)
    tile_event(3, 0, 0)
    col_event(2, 1, 1)
    tile_event(3, 0, 1)
    tile_event(3, 0, 2)
    col_far_event(0)
    tile_event(2, 1, 0)
    tile_event(2, 1, 1)
    col_far_event(1)

    def group(owner_z, core, add):
        for owner_x in range(2):
            row = row_of(owner_z, owner_x, core)
            first = ((owner_z * 2 + owner_x) * 2 + core) * OWN
            index = (owner_z * 2 + owner_x) * OWN
            slots = [sscal[row, 0, j] for j in range(OWN)]
            left = [hid_t[slot // MODEL] for slot in slots]
            right = [cbuf[lax.rem(slot, MODEL)] for slot in slots]
            dots = [jnp.dot(a, b, preferred_element_type=F32) for a, b in zip(left, right)]
            for j in range(OWN):
                term = dots[j] * jnp.where(first + j < live, SCALE, 0.0)
                if add:
                    term += tsib[index + j].astype(F32)
                terms[core * 48 + index + j] = term.astype(BF)

    def for_sibling(n):
        owner_z = at(z, FAR_FIRST[n])
        group(owner_z, 1 - c, False)
        traffic.send(
            "T", n, terms.at[pl.ds((1 - c) * 48 + owner_z * 6, 6)], tsib.at[pl.ds(owner_z * 6, 6)], on_core
        )

    def for_own(n):
        traffic.arrive("T", n, tsib.at[pl.ds(0, 6)])
        group(at(z, FAR_FIRST[n]), c, True)

    class Scatter:
        def __init__(self, family, count, local, recv, first, index, pos, on_ring, on_x):
            self.family, self.count, self.local, self.recv, self.first = family, count, local, recv, first
            self.index, self.pos, self.on_ring, self.on_x = index, pos, on_ring, on_x

        def mine(self, step, part, i):
            return self.local.at[self.index(at(self.pos, step), part, i)]

        def like(self, n):
            return self.local.at[pl.ds(0, n)]

        def to_x(self, n):
            for i in range(self.count):
                traffic.send(
                    self.family, ("first", n, i), self.mine((4, 3, -3)[n], 0, i), self.first.at[n, pl.ds(i, 1)], self.on_x
                )

        def from_x(self, n):
            for i in range(self.count):
                traffic.arrive(self.family, ("first", n, i), self.like(1))
                mine = self.mine((4, 3, -3)[n], 1, i)
                mine[...] = (mine[...].astype(F32) + self.first[n, pl.ds(i, 1)].astype(F32)).astype(BF)

        def place(self, way, k, part, i):
            return self.recv.at[0 if way == 1 else 1, k, part, pl.ds(i, 1)]

        def send(self, way, k, part, i, src):
            traffic.send(self.family, (k, part, i), src, self.place(way, k, part, i), self.on_ring(way))

        def fresh(self, k, part):
            for i in range(self.count):
                far = half_way(self.count, i)
                for way in {0: (far,), 1: (-far,), 2: DIRS}[k]:
                    self.send(way, k, part, i, self.mine(way * (4 - k), part, i))

        def event(self, k, part, i):
            ways = (half_way(self.count, i),) if k == 0 else DIRS
            traffic.arrive(self.family, (k, part, i), self.like(len(ways)))
            if k < 3:
                for way in ways:
                    held = self.place(way, k, part, i)
                    held[...] = (held[...].astype(F32) + self.mine(way * (3 - k), part, i)[...].astype(F32)).astype(BF)
                    self.send(way, k + 1, part, i, held)

        def total(self, part, i):
            return (
                self.place(1, 3, part, i)[...].astype(F32)
                + self.place(-1, 3, part, i)[...].astype(F32)
                + self.mine(0, part, i)[...].astype(F32)
            )

        def hand_over(self, i, dst):
            mine = self.mine(0, 0, i)
            mine[...] = self.total(0, i).astype(BF)
            traffic.send(self.family, ("x", i), mine, dst.at[pl.ds(i, 1)], self.on_x)

        def whole(self, i, dst):
            traffic.arrive(self.family, ("x", i), self.like(1))
            return (self.total(1, i) + dst[pl.ds(i, 1)].astype(F32))[0]

    def z_local(pos, part, i):
        which = 1 - xh if part == 0 else xh
        return pl.ds(c * 48 + (pos * 2 + which) * OWN + i, 1)

    def y_local(pos, part, i):
        which = 1 - xl if part == 0 else xl
        return pl.ds((which * RING + pos) * 2 + i, 1)

    grads = Scatter("D", OWN, terms, zrecv, zfirst, z_local, z, on_z, on_x_hi)
    sums = Scatter("B", 2, pbuf, yrecv, yfirst, y_local, y, on_y, on_x_lo)

    for n in range(3):
        for_sibling(n)
    tile_event(2, 1, 2)
    for n in range(3):
        for_own(n)
        grads.to_x(n)
    tile_far_event(0)
    for_sibling(3)
    for_sibling(4)
    tile_far_event(1)
    tile_far_event(2)
    for_own(3)
    for_own(4)
    grads.fresh(2, 0)
    for n in range(5, 8):
        for_sibling(n)
    for n in range(5, 8):
        for_own(n)
    to_inv.wait()
    traffic.arrive("K", 0, wbuf.at[pl.ds(0, 48)])

    def weight(h, m):
        p = h * MODEL + m
        return wbuf[inv[p // EDGE, lax.rem(p, EDGE)]]

    def panel(h, m, count):
        return jnp.concatenate(
            [jnp.concatenate([weight(h + i, m), weight(h + i, m + 1)], axis=1) for i in range(count)], axis=0
        )

    def forward_of(step, part):
        which = 1 - xl if part == 0 else xl
        m = (which * RING + at(y, step)) * 2
        total = jnp.dot(hid[:, 6 * EDGE :], panel(6, m, 1), preferred_element_type=F32)
        for h in (0, 2, 4):
            total += jnp.dot(hid[:, h * EDGE : (h + 2) * EDGE], panel(h, m, 2), preferred_element_type=F32)
        pbuf[m] = total[:, :EDGE].astype(BF)
        pbuf[m + 1] = total[:, EDGE:].astype(BF)

    def backward(h, count):
        def columns(i, total):
            m = i * 2
            left = jnp.concatenate([cbuf[m], cbuf[m + 1]], axis=1)
            return total + lax.dot_general(
                left, panel(h, m, count), (((1,), (1,)), ((), ())), preferred_element_type=F32
            )

        grad = lax.fori_loop(0, MODEL // 2, columns, jnp.zeros((EDGE, count * EDGE), F32), unroll=2)
        piece = slice(h * EDGE, (h + count) * EDGE)
        gate_val, up_val, sig = sigmoid_parts(gate_ref[:, piece], up_ref[:, piece])
        gate_out[:, piece] = (grad * up_val * sig * (1.0 + gate_val * (1.0 - sig))).astype(BF)
        up_out[:, piece] = (grad * (gate_val * sig)).astype(BF)

    for n in range(3):
        forward_of((4, 3, -3)[n], 0)
        sums.to_x(n)
    for n in range(3):
        grads.from_x(n)
        if n == 0:
            grads.fresh(0, 1)
    grads.fresh(1, 1)
    forward_of(2, 0)
    forward_of(-2, 0)
    sums.fresh(2, 0)
    for i in range(OWN):
        grads.event(2, 0, i)
    forward_of(4, 1)
    forward_of(3, 1)
    forward_of(-3, 1)
    for n in range(3):
        sums.from_x(n)
        if n == 0:
            sums.fresh(0, 1)
    sums.fresh(1, 1)
    for i in range(OWN):
        grads.event(0, 1, i)
    forward_of(1, 0)
    forward_of(-1, 0)
    for i in range(2):
        sums.event(2, 0, i)
    forward_of(2, 1)
    forward_of(-2, 1)
    for i in range(OWN):
        grads.event(3, 0, i)
        grads.hand_over(i, xrecv)
    for i in range(2):
        sums.event(0, 1, i)
    forward_of(0, 0)
    forward_of(1, 1)
    backward(2, 2)
    for i in range(OWN):
        grads.event(1, 1, i)
    for i in range(2):
        sums.event(3, 0, i)
        sums.hand_over(i, lrecv)
    forward_of(-1, 1)
    for i in range(2):
        sums.event(1, 1, i)
    forward_of(0, 1)
    backward(0, 2)
    for i in range(OWN):
        grads.event(2, 1, i)
    for i in range(2):
        sums.event(2, 1, i)
    backward(4, 2)
    backward(6, 1)
    for i in range(OWN):
        grads.event(3, 1, i)
    for i in range(2):
        sums.event(3, 1, i)
        proj_ref[:, i * EDGE : (i + 1) * EDGE] = sums.whole(i, lrecv).astype(BF)
    stores = [
        pltpu.make_async_copy(gate_out, gate_out_hbm, lsem.at[0]),
        pltpu.make_async_copy(up_out, up_out_hbm, lsem.at[1]),
        pltpu.make_async_copy(proj_ref, proj_hbm, lsem.at[2]),
        pltpu.make_async_copy(tile_out, tile_hbm, lsem.at[3]),
    ]
    for store in stores[:3]:
        store.start()
    traffic.left("S", rows(0, 7 + 8 + 16))
    traffic.left("A", wbuf.at[pl.ds(0, 45)])
    traffic.left("K", wbuf.at[pl.ds(0, 48)])
    traffic.left("C", cbuf.at[pl.ds(0, 30)])
    traffic.left("T", tsib.at[pl.ds(0, 48)])
    traffic.left("B", pbuf.at[pl.ds(0, 30)])
    for i in range(OWN):
        tile_out[0, i] = grads.whole(i, xrecv)
    stores[3].start()
    traffic.left("D", terms.at[pl.ds(0, 45)])
    for store in stores:
        store.wait()


def hand_out(*refs):
    n = (len(refs) - 1) // 3
    given, out, held, sems = refs[:n], refs[n : 2 * n], refs[2 * n : 3 * n], refs[-1]
    loads = [pltpu.make_async_copy(given[i], held[i], sems.at[0, i]) for i in range(n)]
    stores = [pltpu.make_async_copy(held[i], out[i], sems.at[1, i]) for i in range(n)]
    for load in loads:
        load.start()
    for load, store in zip(loads, stores):
        load.wait()
        store.start()
    for store in stores:
        store.wait()


def per_device(gate_pre, up_pre, cotangent, weight_tiles, tile_slots, live_counts):
    smem = pl.BlockSpec(memory_space=pltpu.SMEM)
    hbm = pl.BlockSpec(memory_space=pl.ANY)
    tile = (EDGE, EDGE)
    shapes = (
        jax.ShapeDtypeStruct(cotangent.shape, BF),
        jax.ShapeDtypeStruct(gate_pre.shape, BF),
        jax.ShapeDtypeStruct(up_pre.shape, BF),
        jax.ShapeDtypeStruct(weight_tiles.shape, F32),
    )
    results = pl.pallas_call(
        kernel,
        out_shape=shapes,
        in_specs=[hbm] * 4 + [smem] * 2,
        out_specs=(hbm,) * 4,
        scratch_shapes=[
            *[pltpu.VMEM(shape.shape, shape.dtype) for shape in shapes],
            pltpu.VMEM(gate_pre.shape, BF),
            pltpu.VMEM(up_pre.shape, BF),
            pltpu.VMEM((SLOTS + 1, *tile), BF),
            pltpu.VMEM((MODEL, *tile), BF),
            pltpu.VMEM((SLOTS // OWN, 1, EDGE), jnp.int32),
            pltpu.SMEM((SLOTS // OWN, 1, EDGE), jnp.int32),
            pltpu.VMEM((8, EDGE), jnp.int32),
            pltpu.SMEM((8, EDGE), jnp.int32),
            pltpu.VMEM((EDGE, HID * EDGE), BF),
            pltpu.VMEM((HID, *tile), BF),
            pltpu.VMEM((SLOTS, *tile), BF),
            pltpu.VMEM((SLOTS // 2, *tile), BF),
            pltpu.VMEM((2, 4, 2, OWN, *tile), BF),
            pltpu.VMEM((OWN, *tile), BF),
            pltpu.VMEM((MODEL, *tile), BF),
            pltpu.VMEM((2, 4, 2, 2, *tile), BF),
            pltpu.VMEM((2, *tile), BF),
            pltpu.VMEM((3, OWN, *tile), BF),
            pltpu.VMEM((3, 2, *tile), BF),
            pltpu.SemaphoreType.DMA((SEND_SEMS,)),
            pltpu.SemaphoreType.DMA((RECV_SEMS,)),
            pltpu.SemaphoreType.DMA((5,)),
        ],
        compiler_params=pltpu.CompilerParams(
            collective_id=0, has_side_effects=True, vmem_limit_bytes=VMEM_BYTES
        ),
    )(gate_pre, up_pre, cotangent, weight_tiles, tile_slots, live_counts)
    return pl.pallas_call(
        hand_out,
        out_shape=shapes,
        in_specs=[hbm] * 4,
        out_specs=(hbm,) * 4,
        scratch_shapes=[pltpu.VMEM(shape.shape, shape.dtype) for shape in shapes] + [pltpu.SemaphoreType.DMA((2, 4))],
        compiler_params=pltpu.CompilerParams(vmem_limit_bytes=VMEM_BYTES),
    )(*results)


def solution(mesh):
    in_specs = (
        P("dp", "tensor"),
        P("dp", "tensor"),
        P("dp", "tensor"),
        P("tensor", "dp", None, None),
        P("tensor", "dp"),
        P("tensor"),
    )
    out_specs = (
        P("dp", "tensor"),
        P("dp", "tensor"),
        P("dp", "tensor"),
        P("tensor", "dp", None, None),
    )
    return jax.shard_map(
        per_device, mesh=mesh, in_specs=in_specs, out_specs=out_specs, check_vma=False
    )
```
